32 devices in a mesh: cube: 4 (over y, x), blk: 8 (over z, core).
Axes of the slice: x: 2, y: 2, z: 4, core: 2. Of those that a mesh axis runs over, the one named last changes fastest.
Arguments:
- updates: float32 [4, 8, 8, 128, 128], P('cube', 'blk'), may hold values from -6 to 6
- pivot_panel: float32 [2048, 256], P(('cube', 'blk')), may hold values from -1.5 to 1.5
- map_low: int32 [4, 8, 8], P('cube', 'blk'), may hold values from 0 to 7
- map_own: int32 [4, 8, 8], P('cube', 'blk'), may hold values from 0 to 7
- map_out: int32 [4, 8, 8], P('cube', 'blk'), may hold values from 0 to 7
Outputs:
- schur: float32 [4, 8, 64, 2048], P(None, 'blk', None, 'cube')
The draws below stay inside these ranges and needn't reach their ends.
All inputs are finite; a program needn't handle non-finite values.
Results may differ from the reference program's by a relative error of at most 0.000058.
Values sent between devices are 32-bit elements; how exact they have to be, the bound alone decides.
No kernel may reach another device: no remote copies, remote signals or barrier semaphores. Data moves between devices by JAX's collectives and lax.ppermute only.
A program may use at most 64 MiB of HBM per device.

```python
import jax
import jax.numpy as jnp
import numpy as np
from jax import lax

PR = 64
UB = 8
BS = 128
PANEL = 256
M = 2048
TB = 8
N_CUBE = 4
N_BLK = 8


def touch_ends(values, stream_key, low, high):
    shape = values.shape
    place = [jax.random.randint(jax.random.fold_in(stream_key, axis), (), 0, shape[axis]) for axis in range(len(shape))]
    values = values.at[tuple(place)].set(low)
    longest = shape.index(max(shape))
    place[longest] = (place[longest] + 1) % shape[longest]
    return values.at[tuple(place)].set(high)


def steps_of(own_key, extent, shards, smallest, high):
    gain = 1.0
    for axis_at, shards_of in shards:
        steps = jax.random.uniform(jax.random.fold_in(jax.random.fold_in(own_key, 6), axis_at), (shards_of,), jnp.float32, smallest / len(shards), high / len(shards))
        gain = gain * jnp.repeat(jnp.exp(steps), extent[axis_at] // shards_of).reshape((-1,) + (1,) * (len(extent) - 1 - axis_at))
    return gain


def normal_values(own_key, shape, scale, bound, shards=(), kind=jnp.bfloat16):
    entries = jax.random.normal(own_key, shape, jnp.float32) * scale
    if len(shards) > 0:
        entries = steps_of(own_key, shape, shards, -0.22, 0.18) * entries
    return jnp.clip(entries, min=-bound, max=bound).astype(kind)


def setup_inputs(seed: int = 0) -> dict:
    streams_of = jax.random.split(jax.random.key(seed), 6)
    updates = normal_values(streams_of[0], (N_CUBE, N_BLK, UB, BS, BS), 1.0, 6.0, ((0, 4), (1, 8)), jnp.float32)
    pivot_panel = normal_values(streams_of[1], (M, PANEL), 0.25, 1.5, ((0, 32),), jnp.float32)
    map_low = touch_ends(jax.random.randint(streams_of[2], (N_CUBE, N_BLK, UB), 0, UB), jax.random.fold_in(streams_of[2], 1), 0, UB - 1).astype(jnp.int32)
    map_own = touch_ends(jax.random.randint(streams_of[3], (N_CUBE, N_BLK, UB), 0, TB), jax.random.fold_in(streams_of[3], 1), 0, TB - 1).astype(jnp.int32)
    map_out = touch_ends(jax.random.randint(streams_of[4], (N_CUBE, N_BLK, UB), 0, TB), jax.random.fold_in(streams_of[4], 1), 0, TB - 1).astype(jnp.int32)
    return {"updates": updates, "pivot_panel": pivot_panel, "map_low": map_low, "map_own": map_own, "map_out": map_out}


exact_mode = lax.Precision.HIGHEST


def one_hot(targets, classes):
    return (targets[..., None] == jnp.arange(classes, dtype=jnp.int32)).astype(jnp.float32)


def reference(updates, pivot_panel, map_low, map_own, map_out):
    bit_count = N_CUBE.bit_length() - 1
    cube_ids = np.arange(N_CUBE)
    low_peer = cube_ids ^ (1 << (bit_count - 2))
    top_peer = cube_ids ^ (1 << (bit_count - 1))
    blocks = updates.reshape(N_CUBE, N_BLK, UB, BS * BS)
    outgoing = jnp.einsum("cbus,cbuk->cbsk", one_hot(map_low, UB), blocks, precision=exact_mode)
    merged = blocks + outgoing[low_peer]
    own_part = jnp.einsum("cbst,cbsk->cbtk", one_hot(map_own, TB), merged, precision=exact_mode)
    peer_part = jnp.einsum("cbst,cbsk->cbtk", one_hot(map_out, TB), merged, precision=exact_mode)
    tile_sums = own_part + peer_part[top_peer]
    row_count = N_CUBE * PR
    col_count = N_BLK * PR
    tile_grid = tile_sums.reshape(N_CUBE, N_BLK, row_count // BS, col_count // BS, BS, BS)
    tile_grid = tile_grid.transpose(0, 1, 2, 4, 3, 5).reshape(N_CUBE, N_BLK, N_CUBE, PR, col_count)
    front_block = tile_grid.transpose(2, 1, 3, 0, 4).reshape(N_CUBE, N_BLK, PR, N_CUBE * col_count)
    row_panel = pivot_panel.reshape(N_CUBE, N_BLK, PR, PANEL)
    product = jnp.einsum("abkp,jp->abkj", row_panel, pivot_panel, precision=exact_mode)
    return front_block - product
```

```python
import functools

import jax
import jax.numpy as jnp
from jax import lax
from jax.experimental import pallas as pl
from jax.experimental.pallas import tpu as pltpu
from jax.sharding import PartitionSpec as P

AXES = ("cube", "blk")
VMEM = pl.BlockSpec(memory_space=pltpu.VMEM)
SMEM = pl.BlockSpec(memory_space=pltpu.SMEM)


class Plan:
    def __init__(self, tile_count, block_count):
        self.cubes, self.blks = lax.axis_size("cube"), lax.axis_size("blk")
        bit_count = self.cubes.bit_length() - 1
        self.low, self.up = 1 << (bit_count - 2), 1 << (bit_count - 1)
        self.balanced = tile_count <= block_count

    def turned(self, b):
        return self.balanced and b % 2 == 1

    def offset(self, b, stage):
        return self.up if self.turned(b) == (stage == 0) else self.low

    def swap(self, shard, stage):
        pairs = [
            (c * self.blks + b, (c ^ self.offset(b, stage)) * self.blks + b)
            for c in range(self.cubes)
            for b in range(self.blks)
        ]
        return lax.ppermute(shard, AXES, pairs)

    def is_turned(self):
        return lax.rem(lax.axis_index("blk"), 2) == 1 if self.balanced else jnp.bool_(False)


def flipped(shard, axis, offset):
    return lax.ppermute(shard, axis, [(i, i ^ offset) for i in range(lax.axis_size(axis))])


def send_kernel(plan, block_count, low, out, low_met, own_other, out_far, mine, met, sent):
    turned = plan.is_turned()
    sent[...] = jnp.zeros_like(sent)
    for u in range(block_count):
        if plan.balanced:
            slot = jnp.where(turned, own_other[0, 0, low[0, 0, u]], out[0, 0, u])
        else:
            slot = u
        sent[slot] += mine[0, 0, u]
    for u in range(block_count):
        slot = low_met[0, 0, u]
        if plan.balanced:
            slot = jnp.where(turned, out_far[0, 0, slot], out[0, 0, slot])
        sent[slot] += met[0, 0, u]


def part_kernel(plan, block_count, row_offsets, col_offsets, own, low_met, out_met, *refs):
    rows, cols = len(row_offsets), len(col_offsets)
    mine, met = refs[:2]
    row_refs, col_refs = refs[2 : 2 + rows], refs[2 + rows : 2 + rows + cols]
    part, tiles, left, right = refs[2 + rows + cols :]
    part_rows = row_refs[0].shape[0]
    turned = plan.is_turned()
    tiles[...] = jnp.zeros_like(tiles)
    for u in range(block_count):
        tiles[own[0, 0, u]] += mine[0, 0, u]
    for u in range(block_count):
        slot = own[0, 0, low_met[0, 0, u]]
        if plan.balanced:
            slot = jnp.where(turned, out_met[0, 0, u], slot)
        tiles[slot] += met[0, 0, u]
    c, b = lax.axis_index("cube"), lax.axis_index("blk")
    for ref, (straight, crossed) in zip(row_refs, row_offsets):
        at = lax.bitwise_xor(c, jnp.where(turned, jnp.int32(crossed), jnp.int32(straight)))
        left[pl.ds(pl.multiple_of(at * part_rows, part_rows), part_rows), :] = ref[...]
    for ref, offset in zip(col_refs, col_offsets):
        at = lax.bitwise_xor(b, jnp.int32(offset))
        right[pl.ds(pl.multiple_of(at * part_rows, part_rows), part_rows), :] = ref[...]
    size = tiles.shape[1]
    across = right.shape[0] // size

    @pl.loop(0, left.shape[0] // size)
    def _(i):
        panel = left[pl.ds(pl.multiple_of(i * size, size), size), :]
        for j in range(across):
            product = lax.dot_general(
                panel,
                right[j * size : (j + 1) * size, :],
                (((1,), (1,)), ((), ())),
                precision=lax.Precision.HIGHEST,
                preferred_element_type=jnp.float32,
            )
            part[pl.ds(pl.multiple_of(i * size, size), size), j * size : (j + 1) * size] = (
                tiles[i * across + j] - product
            )


def last_kernel(plan, block_count, out_other, part, got, result, *scratch):
    size = got.shape[-1]
    across = result.shape[1] // size
    tiles = got
    if not plan.balanced:
        tiles = scratch[0]
        tiles[...] = jnp.zeros_like(tiles)
        for u in range(block_count):
            tiles[out_other[0, 0, u]] += got[u]
    for t in range(tiles.shape[0]):
        i, j = t // across, t % across
        at = (slice(i * size, (i + 1) * size), slice(j * size, (j + 1) * size))
        result[at] = part[at] + tiles[t]


def local(updates, pivot_panel, map_low, map_own, map_out):
    block_count, size = updates.shape[2], updates.shape[3]
    part_rows, depth = pivot_panel.shape
    row_count = lax.axis_size("cube") * part_rows
    col_count = lax.axis_size("blk") * part_rows
    tile_count = row_count // size * (col_count // size)
    plan = Plan(tile_count, block_count)
    f32 = jnp.float32

    met = plan.swap(updates, 0)
    low_met, out_met = plan.swap(map_low, 0), plan.swap(map_out, 0)
    own_other, out_other = plan.swap(map_own, 1), plan.swap(map_out, 1)
    out_far = plan.swap(out_met, 1)

    s0, s1 = (plan.offset(0, 0), plan.offset(1, 0)), (plan.offset(0, 1), plan.offset(1, 1))
    near = plan.swap(pivot_panel, 0)
    row_panels = [pivot_panel, near, plan.swap(pivot_panel, 1), plan.swap(near, 1)]
    row_offsets = [(0, 0), s0, s1, (s0[0] ^ s1[0], s0[1] ^ s1[1])]
    for offset in [1 << k for k in range(plan.cubes.bit_length() - 1)]:
        if offset not in (plan.low, plan.up):
            row_panels += [flipped(p, "cube", offset) for p in row_panels]
            row_offsets += [(a ^ offset, d ^ offset) for a, d in row_offsets]
    col_offsets = list(range(0, plan.blks, 2))
    col_panels = [pivot_panel if o == 0 else flipped(pivot_panel, "blk", o) for o in col_offsets]
    col_panels += [flipped(p, "blk", 1) for p in col_panels]
    col_offsets += [o + 1 for o in col_offsets]

    sent = pl.pallas_call(
        functools.partial(send_kernel, plan, block_count),
        out_shape=jax.ShapeDtypeStruct((block_count, size, size), f32),
        in_specs=[SMEM] * 5 + [VMEM] * 2,
        out_specs=VMEM,
        compiler_params=pltpu.CompilerParams(vmem_limit_bytes=16 << 20),
        cost_estimate=pl.CostEstimate(flops=1 << 18, bytes_accessed=3 << 19, transcendentals=0),
        name="send",
    )(map_low, map_out, low_met, own_other, out_far, updates, met)
    got = plan.swap(sent, 1)

    part = pl.pallas_call(
        functools.partial(part_kernel, plan, block_count, row_offsets, col_offsets),
        out_shape=jax.ShapeDtypeStruct((row_count, col_count), f32),
        in_specs=[SMEM] * 3 + [VMEM] * (2 + len(row_panels) + len(col_panels)),
        out_specs=VMEM,
        scratch_shapes=[
            pltpu.VMEM((tile_count, size, size), f32),
            pltpu.VMEM((row_count, depth), f32),
            pltpu.VMEM((col_count, depth), f32),
        ],
        compiler_params=pltpu.CompilerParams(vmem_limit_bytes=40 << 20),
        cost_estimate=pl.CostEstimate(
            flops=12 * row_count * col_count * depth, bytes_accessed=1 << 21, transcendentals=0
        ),
        name="part",
    )(map_own, low_met, out_met, updates, met, *row_panels, *col_panels)

    result = pl.pallas_call(
        functools.partial(last_kernel, plan, block_count),
        out_shape=jax.ShapeDtypeStruct((row_count, col_count), f32),
        in_specs=[SMEM, VMEM, VMEM],
        out_specs=VMEM,
        scratch_shapes=[] if plan.balanced else [pltpu.VMEM((tile_count, size, size), f32)],
        compiler_params=pltpu.CompilerParams(vmem_limit_bytes=40 << 20),
        cost_estimate=pl.CostEstimate(flops=1 << 18, bytes_accessed=3 << 19, transcendentals=0),
        name="last",
    )(out_other, part, got)
    return result.reshape(lax.axis_size("cube"), 1, part_rows, col_count)


def solution(mesh):
    placed = (
        P("cube", "blk", None, None, None),
        P(("cube", "blk"), None),
        P("cube", "blk", None),
        P("cube", "blk", None),
        P("cube", "blk", None),
    )
    return jax.shard_map(
        local, mesh=mesh, in_specs=placed, out_specs=P(None, "blk", None, "cube"), check_vma=False
    )
```

```python
import functools

import jax
import jax.numpy as jnp
from jax import lax
from jax.experimental import pallas as pl
from jax.experimental.pallas import tpu as pltpu
from jax.sharding import PartitionSpec as P

AXES = ("cube", "blk")
VMEM = pl.BlockSpec(memory_space=pltpu.VMEM)
SMEM = pl.BlockSpec(memory_space=pltpu.SMEM)
ROW, COL = "row", "col"
LINES, LANES = 8, 128
LOW, OWN, OUT, OTHER = 0, 1, 2, 3
f32, i32 = jnp.float32, jnp.int32
COST = dict(hint=1 << 33, label=0, pack=0, pair=0, send=1 << 30, merge=0, part=1 << 31, last=0)


class Plan:
    def __init__(self, updates, pivot_panel):
        self.slots, self.size = updates.shape[2], updates.shape[3]
        self.part_rows, self.depth = pivot_panel.shape
        self.cubes, self.blks = lax.axis_size("cube"), lax.axis_size("blk")
        self.rows, self.cols = self.cubes * self.part_rows, self.blks * self.part_rows
        self.across = self.cols // self.size
        self.tiles = self.rows // self.size * self.across
        bit_count = self.cubes.bit_length() - 1
        self.low, self.up = 1 << (bit_count - 2), 1 << (bit_count - 1)
        self.balanced = self.tiles <= self.slots

    def offset(self, b, stage):
        turned = self.balanced and b % 2 == 1
        return self.up if turned == (stage == 0) else self.low

    def move(self, shard, even, odd):
        pairs = []
        for c in range(self.cubes):
            for b in range(self.blks):
                if (odd if b % 2 else even) is None:
                    continue
                dc, db = odd if b % 2 else even
                pairs.append((c * self.blks + b, (c ^ dc) * self.blks + (b ^ db)))
        return lax.ppermute(shard, AXES, pairs)

    def swap(self, shard, stage):
        return self.move(shard, (self.offset(0, stage), 0), (self.offset(1, stage), 0))

    def is_odd(self):
        return lax.rem(lax.axis_index("blk"), 2) == 1


def call(kernel, outs, in_specs, args, name, scratch=(), limit=8):
    return pl.pallas_call(
        kernel,
        out_shape=outs,
        in_specs=in_specs,
        out_specs=[VMEM] * len(outs) if isinstance(outs, list) else VMEM,
        scratch_shapes=list(scratch),
        compiler_params=pltpu.CompilerParams(vmem_limit_bytes=limit << 20),
        cost_estimate=pl.CostEstimate(flops=COST[name], bytes_accessed=0, transcendentals=0),
        name=name,
    )(*args)


def hint_kernel(mark):
    mark[...] = jnp.zeros_like(mark)


def label_kernel(n, mark, panel, low, own, out, labelled):
    labelled[0:n] = panel[...]
    labelled[n:] = jnp.zeros((LINES, labelled.shape[1]), f32)
    for line, ref in ((LOW, low), (OWN, own), (OUT, out)):
        labelled[n + line : n + line + 1, 0 : ref.shape[2]] = ref[0].astype(f32)


def pair_kernel(n, mark, own, other, joined):
    joined[0:n] = own[...]
    joined[n : 2 * n] = other[...]


def pack_kernel(n, after, labelled, other, panels, maps):
    panels[0:n] = labelled[0:n]
    panels[n : 2 * n] = other[0:n]
    maps[...] = jnp.zeros_like(maps)
    maps[0:3] = labelled[n : n + 3, 0:LANES].astype(i32)
    maps[3:6] = other[n : n + 3, 0:LANES].astype(i32)


def merge_kernel(n, after, also, along, next_to, joined):
    joined[0 : 2 * n] = along[...]
    joined[2 * n : 3 * n] = next_to[...]


def send_kernel(plan, maps, maps_met, mine, met, sent):
    if not plan.balanced:
        sent[...] = mine[0, 0]
        for u in range(plan.slots):
            sent[maps_met[LOW, u]] += met[0, 0, u]
        return
    odd = plan.is_odd()
    sent[...] = jnp.zeros_like(sent)
    for u in range(plan.slots):
        slot = jnp.where(odd, maps[OTHER + OWN, maps[LOW, u]], maps[OUT, u])
        sent[slot] += mine[0, 0, u]
    for u in range(plan.slots):
        slot = maps_met[LOW, u]
        slot = jnp.where(odd, maps_met[OTHER + OUT, slot], maps[OUT, slot])
        sent[slot] += met[0, 0, u]


def part_kernel(plan, places, maps, maps_met, mine, met, *refs):
    part, tiles, left, right = refs[-4:]
    n, size = plan.part_rows, plan.size
    odd = plan.is_odd()
    tiles[...] = jnp.zeros_like(tiles)
    for u in range(plan.slots):
        tiles[maps[OWN, u]] += mine[0, 0, u]
    for u in range(plan.slots):
        slot = maps[OWN, maps_met[LOW, u]]
        if plan.balanced:
            slot = jnp.where(odd, maps_met[OUT, u], slot)
        tiles[slot] += met[0, 0, u]

    def lay(parity):
        for ref, chunks in zip(refs, places[parity]):
            for k, (kind, offset) in ((k, place) for k, chunk in enumerate(chunks) for place in chunk):
                to, me = (left, lax.axis_index("cube")) if kind == ROW else (right, lax.axis_index("blk"))
                at = lax.bitwise_xor(me, i32(offset))
                to[pl.ds(pl.multiple_of(at * n, n), n), :] = ref[k * n : (k + 1) * n]

    if places[0] == places[1]:
        lay(0)
    else:
        pl.when(jnp.logical_not(odd))(functools.partial(lay, 0))
        pl.when(odd)(functools.partial(lay, 1))

    @pl.loop(0, plan.rows // size)
    def _(i):
        panel = left[pl.ds(pl.multiple_of(i * size, size), size), :]
        for j in range(plan.across):
            product = lax.dot_general(
                panel,
                right[j * size : (j + 1) * size, :],
                (((1,), (1,)), ((), ())),
                precision=lax.Precision.HIGHEST,
                preferred_element_type=f32,
            )
            part[pl.ds(pl.multiple_of(i * size, size), size), j * size : (j + 1) * size] = (
                tiles[i * plan.across + j] - product
            )


def last_kernel(plan, *refs):
    size, across = plan.size, plan.across
    if plan.balanced:
        part, tiles, result = refs
    else:
        maps, part, got, result, tiles = refs
        tiles[...] = jnp.zeros_like(tiles)
        for u in range(plan.slots):
            tiles[maps[OTHER + OUT, u]] += got[u]
    for t in range(plan.tiles):
        i, j = t // across, t % across
        at = (slice(i * size, (i + 1) * size), slice(j * size, (j + 1) * size))
        result[at] = part[at] + tiles[t]


def after(first, *then):
    return lax.optimization_barrier((first, *then))[1:]


def add_sent(plan, maps, updates, met):
    return call(
        functools.partial(send_kernel, plan),
        jax.ShapeDtypeStruct(updates.shape[2:], f32),
        [SMEM] * len(maps) + [VMEM] * 2,
        (*maps, updates, met),
        "send",
    )


def add_part(plan, places, maps, updates, met, panels):
    return call(
        functools.partial(part_kernel, plan, places),
        jax.ShapeDtypeStruct((plan.rows, plan.cols), f32),
        [SMEM] * 2 + [VMEM] * (2 + len(panels)),
        (*maps, updates, met, *panels),
        "part",
        [
            pltpu.VMEM((plan.tiles, plan.size, plan.size), f32),
            pltpu.VMEM((plan.rows, plan.depth), f32),
            pltpu.VMEM((plan.cols, plan.depth), f32),
        ],
        limit=40,
    )


def add_last(plan, maps, part, got):
    return call(
        functools.partial(last_kernel, plan),
        jax.ShapeDtypeStruct((plan.rows, plan.cols), f32),
        [SMEM] * len(maps) + [VMEM] * 2,
        (*maps, part, got),
        "last",
        [] if plan.balanced else [pltpu.VMEM((plan.tiles, plan.size, plan.size), f32)],
        limit=40,
    )


def any_mesh(plan, updates, pivot_panel, map_low, map_own, map_out):
    met = plan.swap(updates, 0)
    own_maps = jnp.concatenate([map_low[0], map_own[0], map_out[0]])
    maps = jnp.concatenate([own_maps, plan.swap(own_maps, 1)])
    maps_met = plan.swap(maps, 0)
    got = plan.swap(add_sent(plan, [maps, maps_met], updates, met), 1)
    panels, places = [pivot_panel], [[[(ROW, 0), (COL, 0)]]]
    for c in range(1, plan.cubes):
        panels.append(plan.move(pivot_panel, (c, 0), (c, 0)))
        places.append([[(ROW, c)]])
    for b in range(1, plan.blks):
        panels.append(plan.move(pivot_panel, (0, b), (0, b)))
        places.append([[(COL, b)]])
    part = add_part(plan, (places, places), (maps, maps_met), updates, met, panels)
    return add_last(plan, [] if plan.balanced else [maps], part, got)


def four_by_eight(plan, updates, pivot_panel, map_low, map_own, map_out):
    n, depth = plan.part_rows, plan.depth
    shape = jax.ShapeDtypeStruct
    sibling = plan.move(pivot_panel, (0, 1), (0, 1))
    met = plan.swap(updates, 0)
    mark = call(hint_kernel, shape((LINES, LANES), f32), [], (), "hint")
    labelled = call(
        functools.partial(label_kernel, n),
        shape((n + LINES, depth), f32),
        [VMEM] * 5,
        (mark, pivot_panel, map_low, map_own, map_out),
        "label",
    )
    other = plan.swap(labelled, 1)
    pair = call(
        functools.partial(pair_kernel, n),
        shape((2 * n, depth), f32),
        [VMEM] * 3,
        (labelled, pivot_panel, sibling),
        "pair",
    )
    along = plan.move(pair, (0, 4), (0, 6))
    panels, maps = call(
        functools.partial(pack_kernel, n),
        [shape((2 * n, depth), f32), shape((LINES, LANES), i32)],
        [VMEM] * 3,
        (pair, labelled, other),
        "pack",
    )
    maps_met = plan.swap(maps, 0)
    panels_met = plan.swap(panels, 0)

    sent = add_sent(plan, [maps, maps_met], updates, met)
    got = plan.swap(sent, 1)

    (panel_late,) = after(sent, pivot_panel)
    next_to = plan.move(panel_late, (0, 2), (0, 2))
    merged = call(
        functools.partial(merge_kernel, n),
        shape((3 * n, depth), f32),
        [VMEM] * 4,
        (sent, panels_met, along, next_to),
        "merge",
    )
    shared = plan.move(merged, (0, 1), (0, 1))
    (s0, s1), (o0, o1) = ((plan.offset(0, k), plan.offset(1, k)) for k in range(2))
    cols = lambda b: [[(COL, b)], [(COL, b ^ 1)]]
    rows = lambda s, o: [[[(ROW, o)]], [[(ROW, s)], [(ROW, s ^ o)]]]
    own = [[(ROW, 0), (COL, 0)], [(COL, 1)]]
    even = [own, *rows(s0, o0), cols(4) + [[(COL, 2)]], cols(7) + [[(COL, 3)]]]
    odd = [own, *rows(s1, o1), cols(6) + [[(COL, 2)]], cols(5) + [[(COL, 3)]]]
    panels = [pair, other, panels_met, merged, shared]
    part = add_part(plan, (even, odd), (maps, maps_met), updates, met, panels)
    return add_last(plan, [], part, got)


def local(updates, *rest):
    plan = Plan(updates, rest[0])
    known = plan.balanced and plan.cubes == 4 and plan.blks == 8
    result = (four_by_eight if known else any_mesh)(plan, updates, *rest)
    return result.reshape(plan.cubes, 1, plan.part_rows, plan.cols)


def solution(mesh):
    placed = (
        P("cube", "blk", None, None, None),
        P(("cube", "blk"), None),
        P("cube", "blk", None),
        P("cube", "blk", None),
        P("cube", "blk", None),
    )
    return jax.shard_map(
        local, mesh=mesh, in_specs=placed, out_specs=P(None, "blk", None, "cube"), check_vma=False
    )
```

```python
import functools

import jax
import jax.numpy as jnp
from jax import lax
from jax.experimental import pallas as pl
from jax.experimental.pallas import tpu as pltpu
from jax.sharding import PartitionSpec as P

AXES = ("cube", "blk")
VMEM = pl.BlockSpec(memory_space=pltpu.VMEM)
SMEM = pl.BlockSpec(memory_space=pltpu.SMEM)
ROW, COL = "row", "col"
LINES, LANES = 8, 128
LOW, OWN, OUT, OTHER = 0, 1, 2, 3
f32, i32 = jnp.float32, jnp.int32
COST = dict(hint=1 << 33, label=0, pair=0, pack=0, send=1 << 30, mark=34 << 25, merge=0, part=0, last=0)


class Plan:
    def __init__(self, updates, pivot_panel):
        self.slots, self.size = updates.shape[2], updates.shape[3]
        self.part_rows, self.depth = pivot_panel.shape
        self.cubes, self.blks = lax.axis_size("cube"), lax.axis_size("blk")
        self.rows, self.cols = self.cubes * self.part_rows, self.blks * self.part_rows
        self.across = self.cols // self.size
        self.tiles = self.rows // self.size * self.across
        bit_count = self.cubes.bit_length() - 1
        self.low, self.up = 1 << (bit_count - 2), 1 << (bit_count - 1)
        self.balanced = self.tiles <= self.slots

    def offset(self, b, stage):
        turned = self.balanced and b % 2 == 1
        return self.up if turned == (stage == 0) else self.low

    def move(self, shard, even, odd):
        pairs = []
        for c in range(self.cubes):
            for b in range(self.blks):
                if (odd if b % 2 else even) is None:
                    continue
                dc, db = odd if b % 2 else even
                pairs.append((c * self.blks + b, (c ^ dc) * self.blks + (b ^ db)))
        return lax.ppermute(shard, AXES, pairs)

    def swap(self, shard, stage):
        return self.move(shard, (self.offset(0, stage), 0), (self.offset(1, stage), 0))

    def is_odd(self):
        return lax.rem(lax.axis_index("blk"), 2) == 1


def call(kernel, outs, in_specs, args, name, scratch=(), limit=8):
    return pl.pallas_call(
        kernel,
        out_shape=outs,
        in_specs=in_specs,
        out_specs=[VMEM] * len(outs) if isinstance(outs, list) else VMEM,
        scratch_shapes=list(scratch),
        compiler_params=pltpu.CompilerParams(vmem_limit_bytes=limit << 20),
        cost_estimate=pl.CostEstimate(flops=COST[name], bytes_accessed=0, transcendentals=0),
        name=name,
    )(*args)


def hint_kernel(mark):
    mark[...] = jnp.zeros_like(mark)


def label_kernel(mark, low, own, out, maps):
    maps[...] = jnp.zeros_like(maps)
    for line, ref in ((LOW, low), (OWN, own), (OUT, out)):
        maps[line : line + 1, 0 : ref.shape[2]] = ref[0]


def pair_kernel(n, after, own, other, joined):
    joined[0:n] = own[...]
    joined[n : 2 * n] = other[...]


def pack_kernel(after, own, other, maps):
    maps[...] = jnp.zeros_like(maps)
    maps[0:OTHER] = own[0:OTHER]
    maps[OTHER : 2 * OTHER] = other[0:OTHER]


def merge_kernel(n, after, near, far, along, joined):
    for k, ref in enumerate((along, near, far)):
        joined[2 * n * k : 2 * n * (k + 1)] = ref[...]


def mark_kernel(after, along, mark):
    mark[...] = along[0:LINES, 0:LANES]


def scalars(values, count):
    return [values[0, u] for u in range(count)]


def send_kernel(plan, maps, maps_met, mine, met, sent):
    line = lambda ref, k: jnp.broadcast_to(ref[k : k + 1, :], (LINES, LANES))
    through = lambda targets, slots: jnp.take_along_axis(targets, slots, axis=1, mode="promise_in_bounds")
    if plan.balanced:
        odd = plan.is_odd()
        own_slots = jnp.where(odd, through(line(maps, OTHER + OWN), line(maps, LOW)), line(maps, OUT))
        target = jnp.where(odd, line(maps_met, OTHER + OUT), line(maps, OUT))
        met_slots = through(target, line(maps_met, LOW))
        sent[...] = jnp.zeros_like(sent)
        for u, slot in enumerate(scalars(own_slots, plan.slots)):
            sent[slot] += mine[0, 0, u]
    else:
        met_slots = line(maps_met, LOW)
        sent[...] = mine[0, 0]
    for u, slot in enumerate(scalars(met_slots, plan.slots)):
        sent[slot] += met[0, 0, u]


def part_kernel(plan, places, maps, maps_met, mine, met, *refs):
    part, tiles, left, right = refs[-4:]
    n, size = plan.part_rows, plan.size
    odd = plan.is_odd()
    tiles[...] = jnp.zeros_like(tiles)
    for u in range(plan.slots):
        tiles[maps[OWN, u]] += mine[0, 0, u]
    for u in range(plan.slots):
        slot = maps[OWN, maps_met[LOW, u]]
        if plan.balanced:
            slot = jnp.where(odd, maps_met[OUT, u], slot)
        tiles[slot] += met[0, 0, u]

    def lay(parity):
        for ref, chunks in zip(refs, places[parity]):
            for k, (kind, offset) in ((k, place) for k, chunk in enumerate(chunks) for place in chunk):
                to, me = (left, lax.axis_index("cube")) if kind == ROW else (right, lax.axis_index("blk"))
                at = lax.bitwise_xor(me, i32(offset))
                to[pl.ds(pl.multiple_of(at * n, n), n), :] = ref[k * n : (k + 1) * n]

    if places[0] == places[1]:
        lay(0)
    else:
        pl.when(jnp.logical_not(odd))(functools.partial(lay, 0))
        pl.when(odd)(functools.partial(lay, 1))

    @pl.loop(0, plan.rows // size)
    def _(i):
        panel = left[pl.ds(pl.multiple_of(i * size, size), size), :]
        for j in range(plan.across):
            product = lax.dot_general(
                panel,
                right[j * size : (j + 1) * size, :],
                (((1,), (1,)), ((), ())),
                precision=lax.Precision.HIGHEST,
                preferred_element_type=f32,
            )
            part[pl.ds(pl.multiple_of(i * size, size), size), j * size : (j + 1) * size] = (
                tiles[i * plan.across + j] - product
            )


def last_kernel(plan, *refs):
    size, across = plan.size, plan.across
    if plan.balanced:
        part, tiles, result = refs
    else:
        maps, part, got, result, tiles = refs
        tiles[...] = jnp.zeros_like(tiles)
        for u in range(plan.slots):
            tiles[maps[OTHER + OUT, u]] += got[u]
    for t in range(plan.tiles):
        i, j = t // across, t % across
        at = (slice(i * size, (i + 1) * size), slice(j * size, (j + 1) * size))
        result[at] = part[at] + tiles[t]


def after(first, *then):
    return lax.optimization_barrier((first, *then))[1:]


def add_sent(plan, maps, updates, met):
    return call(
        functools.partial(send_kernel, plan),
        jax.ShapeDtypeStruct(updates.shape[2:], f32),
        [VMEM] * (len(maps) + 2),
        (*maps, updates, met),
        "send",
    )


def add_part(plan, places, maps, updates, met, panels):
    return call(
        functools.partial(part_kernel, plan, places),
        jax.ShapeDtypeStruct((plan.rows, plan.cols), f32),
        [SMEM] * 2 + [VMEM] * (2 + len(panels)),
        (*maps, updates, met, *panels),
        "part",
        [
            pltpu.VMEM((plan.tiles, plan.size, plan.size), f32),
            pltpu.VMEM((plan.rows, plan.depth), f32),
            pltpu.VMEM((plan.cols, plan.depth), f32),
        ],
        limit=40,
    )


def add_last(plan, maps, part, got):
    return call(
        functools.partial(last_kernel, plan),
        jax.ShapeDtypeStruct((plan.rows, plan.cols), f32),
        [SMEM] * len(maps) + [VMEM] * 2,
        (*maps, part, got),
        "last",
        [] if plan.balanced else [pltpu.VMEM((plan.tiles, plan.size, plan.size), f32)],
        limit=40,
    )


def any_mesh(plan, updates, pivot_panel, map_low, map_own, map_out):
    met = plan.swap(updates, 0)
    own_maps = jnp.concatenate([map_low[0], map_own[0], map_out[0]])
    own_maps = jnp.pad(own_maps, ((0, 0), (0, LANES - plan.slots)))
    maps = jnp.concatenate([own_maps, plan.swap(own_maps, 1)])
    maps_met = plan.swap(maps, 0)
    got = plan.swap(add_sent(plan, [maps, maps_met], updates, met), 1)
    panels, places = [pivot_panel], [[[(ROW, 0), (COL, 0)]]]
    for c in range(1, plan.cubes):
        panels.append(plan.move(pivot_panel, (c, 0), (c, 0)))
        places.append([[(ROW, c)]])
    for b in range(1, plan.blks):
        panels.append(plan.move(pivot_panel, (0, b), (0, b)))
        places.append([[(COL, b)]])
    part = add_part(plan, (places, places), (maps, maps_met), updates, met, panels)
    return add_last(plan, [] if plan.balanced else [maps], part, got)


def four_by_eight(plan, updates, pivot_panel, map_low, map_own, map_out):
    n, depth = plan.part_rows, plan.depth
    shape = jax.ShapeDtypeStruct
    met = plan.swap(updates, 0)
    mark = call(hint_kernel, shape((LINES, LANES), f32), [], (), "hint")
    (panel_late,) = after(mark, pivot_panel)
    sibling = plan.move(panel_late, (0, 1), (0, 1))
    lines = shape((LINES, LANES), i32)
    own_maps = call(label_kernel, lines, [VMEM] * 4, (mark, map_low, map_own, map_out), "label")
    other_maps = plan.swap(own_maps, 1)
    pair = call(
        functools.partial(pair_kernel, n),
        shape((2 * n, depth), f32),
        [VMEM] * 3,
        (own_maps, pivot_panel, sibling),
        "pair",
    )
    along = plan.move(pair, (0, 4), (0, 6))
    maps = call(pack_kernel, lines, [VMEM] * 3, (pair, own_maps, other_maps), "pack")
    maps_met = plan.swap(maps, 0)
    (pair_late,) = after(maps, pair)
    x, y = plan.low, plan.up
    near = plan.move(pair_late, (x, 0), (y, 0))
    far = plan.move(pair_late, (x ^ y, 0), (0, 2))

    sent = add_sent(plan, [maps, maps_met], updates, met)
    got = plan.swap(sent, 1)

    mark = call(mark_kernel, shape((LINES, LANES), f32), [VMEM] * 2, (sent, along), "mark")
    far, near, mark = lax.optimization_barrier((far, near, mark))
    merged = call(
        functools.partial(merge_kernel, n),
        shape((6 * n, depth), f32),
        [VMEM] * 4,
        (mark, near, far, along),
        "merge",
    )
    shared = plan.move(merged, (0, 1), (0, 1))
    own = [[(ROW, 0), (COL, 0)], [(COL, 1)]]
    cols = lambda b: [[(COL, b)], [(COL, b ^ 1)]]
    even = [own, cols(4) + [[(ROW, x)], [], [(ROW, x ^ y)], []], cols(7) + [[], [(ROW, y)]] + cols(3)]
    odd = [own, cols(6) + [[(ROW, y)], []] + cols(2), cols(5) + [[], [(ROW, x)], [], [(ROW, x ^ y)]]]
    panels = [pair, merged, shared]
    part = add_part(plan, (even, odd), (maps, maps_met), updates, met, panels)
    return add_last(plan, [], part, got)


def local(updates, *rest):
    plan = Plan(updates, rest[0])
    known = plan.balanced and plan.cubes == 4 and plan.blks == 8
    result = (four_by_eight if known else any_mesh)(plan, updates, *rest)
    return result.reshape(plan.cubes, 1, plan.part_rows, plan.cols)


def solution(mesh):
    placed = (
        P("cube", "blk", None, None, None),
        P(("cube", "blk"), None),
        P("cube", "blk", None),
        P("cube", "blk", None),
        P("cube", "blk", None),
    )
    return jax.shard_map(
        local, mesh=mesh, in_specs=placed, out_specs=P(None, "blk", None, "cube"), check_vma=False
    )
```

```python
import functools

import jax
import jax.numpy as jnp
from jax import lax
from jax.experimental import pallas as pl
from jax.experimental.pallas import tpu as pltpu
from jax.sharding import PartitionSpec as P

AXES = ("cube", "blk")
VMEM = pl.BlockSpec(memory_space=pltpu.VMEM)
SMEM = pl.BlockSpec(memory_space=pltpu.SMEM)
ROW, COL = "row", "col"
LINES, LANES = 8, 128
LOW, OWN, OUT, OTHER = 0, 1, 2, 3
f32, i32 = jnp.float32, jnp.int32
COST = dict(hint=1 << 33, label=0, pair=0, pack=0, send=1 << 30, mark=34 << 25, merge=0, part=0, last=0)


class Plan:
    def __init__(self, updates, pivot_panel):
        self.slots, self.size = updates.shape[2], updates.shape[3]
        self.part_rows, self.depth = pivot_panel.shape
        self.cubes, self.blks = lax.axis_size("cube"), lax.axis_size("blk")
        self.rows, self.cols = self.cubes * self.part_rows, self.blks * self.part_rows
        self.across = self.cols // self.size
        self.tiles = self.rows // self.size * self.across
        bit_count = self.cubes.bit_length() - 1
        self.low, self.up = 1 << (bit_count - 2), 1 << (bit_count - 1)
        self.balanced = self.tiles <= self.slots

    def offset(self, b, stage):
        turned = self.balanced and b % 2 == 1
        return self.up if turned == (stage == 0) else self.low

    def move(self, shard, even, odd):
        pairs = []
        for c in range(self.cubes):
            for b in range(self.blks):
                if (odd if b % 2 else even) is None:
                    continue
                dc, db = odd if b % 2 else even
                pairs.append((c * self.blks + b, (c ^ dc) * self.blks + (b ^ db)))
        return lax.ppermute(shard, AXES, pairs)

    def swap(self, shard, stage):
        return self.move(shard, (self.offset(0, stage), 0), (self.offset(1, stage), 0))

    def is_odd(self):
        return lax.rem(lax.axis_index("blk"), 2) == 1


def call(kernel, outs, in_specs, args, name, scratch=(), limit=8):
    return pl.pallas_call(
        kernel,
        out_shape=outs,
        in_specs=in_specs,
        out_specs=[VMEM] * len(outs) if isinstance(outs, list) else VMEM,
        scratch_shapes=list(scratch),
        compiler_params=pltpu.CompilerParams(vmem_limit_bytes=limit << 20),
        cost_estimate=pl.CostEstimate(flops=COST[name], bytes_accessed=0, transcendentals=0),
        name=name,
    )(*args)


def hint_kernel(mark):
    mark[...] = jnp.zeros_like(mark)


def label_kernel(mark, low, own, out, maps):
    maps[...] = jnp.zeros_like(maps)
    for line, ref in ((LOW, low), (OWN, own), (OUT, out)):
        maps[line : line + 1, 0 : ref.shape[2]] = ref[0]


def pair_kernel(n, after, own, other, joined):
    joined[0:n] = own[...]
    joined[n : 2 * n] = other[...]


def pack_kernel(after, own, other, maps):
    maps[...] = jnp.zeros_like(maps)
    maps[0:OTHER] = own[0:OTHER]
    maps[OTHER : 2 * OTHER] = other[0:OTHER]


def merge_kernel(n, after, near, far, along, joined):
    for k, ref in enumerate((along, near, far)):
        joined[2 * n * k : 2 * n * (k + 1)] = ref[...]


def mark_kernel(after, along, mark):
    mark[...] = along[0:LINES, 0:LANES]


def scalars(values, count):
    return [values[0, u] for u in range(count)]


def send_kernel(plan, maps, maps_met, mine, met, sent):
    line = lambda ref, k: jnp.broadcast_to(ref[k : k + 1, :], (LINES, LANES))
    through = lambda targets, slots: jnp.take_along_axis(targets, slots, axis=1, mode="promise_in_bounds")
    if plan.balanced:
        odd = plan.is_odd()
        own_slots = jnp.where(odd, through(line(maps, OTHER + OWN), line(maps, LOW)), line(maps, OUT))
        target = jnp.where(odd, line(maps_met, OTHER + OUT), line(maps, OUT))
        met_slots = through(target, line(maps_met, LOW))
        sent[...] = jnp.zeros_like(sent)
        for u, slot in enumerate(scalars(own_slots, plan.slots)):
            sent[slot] += mine[0, 0, u]
    else:
        met_slots = line(maps_met, LOW)
        sent[...] = mine[0, 0]
    for u, slot in enumerate(scalars(met_slots, plan.slots)):
        sent[slot] += met[0, 0, u]


def part_kernel(plan, places, maps, maps_met, mine, met, *refs):
    part, tiles, left, right = refs[-4:]
    n, size = plan.part_rows, plan.size
    odd = plan.is_odd()
    tiles[...] = jnp.zeros_like(tiles)
    for u in range(plan.slots):
        tiles[maps[OWN, u]] += mine[0, 0, u]
    for u in range(plan.slots):
        slot = maps[OWN, maps_met[LOW, u]]
        if plan.balanced:
            slot = jnp.where(odd, maps_met[OUT, u], slot)
        tiles[slot] += met[0, 0, u]

    def lay(parity):
        for ref, chunks in zip(refs, places[parity]):
            for k, (kind, offset) in ((k, place) for k, chunk in enumerate(chunks) for place in chunk):
                to, me = (left, lax.axis_index("cube")) if kind == ROW else (right, lax.axis_index("blk"))
                at = lax.bitwise_xor(me, i32(offset))
                to[pl.ds(pl.multiple_of(at * n, n), n), :] = ref[k * n : (k + 1) * n]

    if places[0] == places[1]:
        lay(0)
    else:
        pl.when(jnp.logical_not(odd))(functools.partial(lay, 0))
        pl.when(odd)(functools.partial(lay, 1))

    @pl.loop(0, plan.rows // size)
    def _(i):
        panel = left[pl.ds(pl.multiple_of(i * size, size), size), :]
        for j in range(plan.across):
            product = lax.dot_general(
                panel,
                right[j * size : (j + 1) * size, :],
                (((1,), (1,)), ((), ())),
                precision=lax.Precision.HIGHEST,
                preferred_element_type=f32,
            )
            part[pl.ds(pl.multiple_of(i * size, size), size), j * size : (j + 1) * size] = (
                tiles[i * plan.across + j] - product
            )


def last_kernel(plan, *refs):
    size, across = plan.size, plan.across
    if plan.balanced:
        part, tiles, result = refs
    else:
        maps, part, got, result, tiles = refs
        tiles[...] = jnp.zeros_like(tiles)
        for u in range(plan.slots):
            tiles[maps[OTHER + OUT, u]] += got[u]
    for t in range(plan.tiles):
        i, j = t // across, t % across
        at = (slice(i * size, (i + 1) * size), slice(j * size, (j + 1) * size))
        result[at] = part[at] + tiles[t]


def after(first, *then):
    return lax.optimization_barrier((first, *then))[1:]


def add_sent(plan, maps, updates, met):
    return call(
        functools.partial(send_kernel, plan),
        jax.ShapeDtypeStruct(updates.shape[2:], f32),
        [VMEM] * (len(maps) + 2),
        (*maps, updates, met),
        "send",
    )


def add_part(plan, places, maps, updates, met, panels):
    return call(
        functools.partial(part_kernel, plan, places),
        jax.ShapeDtypeStruct((plan.rows, plan.cols), f32),
        [SMEM] * 2 + [VMEM] * (2 + len(panels)),
        (*maps, updates, met, *panels),
        "part",
        [
            pltpu.VMEM((plan.tiles, plan.size, plan.size), f32),
            pltpu.VMEM((plan.rows, plan.depth), f32),
            pltpu.VMEM((plan.cols, plan.depth), f32),
        ],
        limit=40,
    )


def add_last(plan, maps, part, got):
    return call(
        functools.partial(last_kernel, plan),
        jax.ShapeDtypeStruct((plan.rows, plan.cols), f32),
        [SMEM] * len(maps) + [VMEM] * 2,
        (*maps, part, got),
        "last",
        [] if plan.balanced else [pltpu.VMEM((plan.tiles, plan.size, plan.size), f32)],
        limit=40,
    )


def any_mesh(plan, updates, pivot_panel, map_low, map_own, map_out):
    met = plan.swap(updates, 0)
    own_maps = jnp.concatenate([map_low[0], map_own[0], map_out[0]])
    own_maps = jnp.pad(own_maps, ((0, 0), (0, LANES - plan.slots)))
    maps = jnp.concatenate([own_maps, plan.swap(own_maps, 1)])
    maps_met = plan.swap(maps, 0)
    got = plan.swap(add_sent(plan, [maps, maps_met], updates, met), 1)
    panels, places = [pivot_panel], [[[(ROW, 0), (COL, 0)]]]
    for c in range(1, plan.cubes):
        panels.append(plan.move(pivot_panel, (c, 0), (c, 0)))
        places.append([[(ROW, c)]])
    for b in range(1, plan.blks):
        panels.append(plan.move(pivot_panel, (0, b), (0, b)))
        places.append([[(COL, b)]])
    part = add_part(plan, (places, places), (maps, maps_met), updates, met, panels)
    return add_last(plan, [] if plan.balanced else [maps], part, got)


def four_by_eight(plan, updates, pivot_panel, map_low, map_own, map_out):
    n, depth = plan.part_rows, plan.depth
    shape = jax.ShapeDtypeStruct
    met = plan.swap(updates, 0)
    mark = call(hint_kernel, shape((LINES, LANES), f32), [], (), "hint")
    (panel_late,) = after(mark, pivot_panel)
    sibling = plan.move(panel_late, (0, 1), (0, 1))
    lines = shape((LINES, LANES), i32)
    own_maps = call(label_kernel, lines, [VMEM] * 4, (mark, map_low, map_own, map_out), "label")
    other_maps = plan.swap(own_maps, 1)
    pair = call(
        functools.partial(pair_kernel, n),
        shape((2 * n, depth), f32),
        [VMEM] * 3,
        (own_maps, pivot_panel, sibling),
        "pair",
    )
    along = plan.move(pair, (0, 4), (0, 6))
    maps = call(pack_kernel, lines, [VMEM] * 3, (pair, own_maps, other_maps), "pack")
    maps_met = plan.swap(maps, 0)
    (pair_late,) = after(maps, pair)
    x, y = plan.low, plan.up
    near = plan.move(pair_late, (x, 0), (y, 0))
    far = plan.move(pair_late, (0, 2), (x ^ y, 0))

    sent = add_sent(plan, [maps, maps_met], updates, met)
    got = plan.swap(sent, 1)

    mark = call(mark_kernel, shape((LINES, LANES), f32), [VMEM] * 2, (sent, along), "mark")
    far, near, mark = lax.optimization_barrier((far, near, mark))
    merged = call(
        functools.partial(merge_kernel, n),
        shape((6 * n, depth), f32),
        [VMEM] * 4,
        (mark, near, far, along),
        "merge",
    )
    shared = plan.move(merged, (0, 1), (0, 1))
    own = [[(ROW, 0), (COL, 0)], [(COL, 1)]]
    cols = lambda b: [[(COL, b)], [(COL, b ^ 1)]]
    even = [own, cols(4) + [[(ROW, x)], []] + cols(2), cols(7) + [[], [(ROW, y)], [], [(ROW, x ^ y)]]]
    odd = [own, cols(6) + [[(ROW, y)], [], [(ROW, x ^ y)], []], cols(5) + [[], [(ROW, x)]] + cols(3)]
    panels = [pair, merged, shared]
    part = add_part(plan, (even, odd), (maps, maps_met), updates, met, panels)
    return add_last(plan, [], part, got)


def local(updates, *rest):
    plan = Plan(updates, rest[0])
    known = plan.balanced and plan.cubes == 4 and plan.blks == 8
    result = (four_by_eight if known else any_mesh)(plan, updates, *rest)
    return result.reshape(plan.cubes, 1, plan.part_rows, plan.cols)


def solution(mesh):
    placed = (
        P("cube", "blk", None, None, None),
        P(("cube", "blk"), None),
        P("cube", "blk", None),
        P("cube", "blk", None),
        P("cube", "blk", None),
    )
    return jax.shard_map(
        local, mesh=mesh, in_specs=placed, out_specs=P(None, "blk", None, "cube"), check_vma=False
    )
```

```python
import functools

import jax
import jax.numpy as jnp
from jax import lax
from jax.experimental import pallas as pl
from jax.experimental.pallas import tpu as pltpu
from jax.sharding import PartitionSpec as P

AXES = ("cube", "blk")
VMEM = pl.BlockSpec(memory_space=pltpu.VMEM)
SMEM = pl.BlockSpec(memory_space=pltpu.SMEM)
ROW, COL = "row", "col"
LINES, LANES = 8, 128
LOW, OWN, OUT, OTHER = 0, 1, 2, 3
f32, i32 = jnp.float32, jnp.int32
COST = dict(hint=1 << 33, label=0, pair=0, pack=0, send=1 << 30, tiles=0, mark=34 << 25, merge=0, part=0, last=0)


class Plan:
    def __init__(self, updates, pivot_panel):
        self.slots, self.size = updates.shape[2], updates.shape[3]
        self.part_rows, self.depth = pivot_panel.shape
        self.cubes, self.blks = lax.axis_size("cube"), lax.axis_size("blk")
        self.rows, self.cols = self.cubes * self.part_rows, self.blks * self.part_rows
        self.across = self.cols // self.size
        self.tiles = self.rows // self.size * self.across
        bit_count = self.cubes.bit_length() - 1
        self.low, self.up = 1 << (bit_count - 2), 1 << (bit_count - 1)
        self.balanced = self.tiles <= self.slots

    def offset(self, b, stage):
        turned = self.balanced and b % 2 == 1
        return self.up if turned == (stage == 0) else self.low

    def move(self, shard, even, odd):
        pairs = []
        for c in range(self.cubes):
            for b in range(self.blks):
                if (odd if b % 2 else even) is None:
                    continue
                dc, db = odd if b % 2 else even
                pairs.append((c * self.blks + b, (c ^ dc) * self.blks + (b ^ db)))
        return lax.ppermute(shard, AXES, pairs)

    def swap(self, shard, stage):
        return self.move(shard, (self.offset(0, stage), 0), (self.offset(1, stage), 0))

    def cross(self, shard, stage):
        return self.move(shard, (self.offset(0, stage), 1), (self.offset(1, stage), 1))

    def is_odd(self):
        return lax.rem(lax.axis_index("blk"), 2) == 1


def call(kernel, outs, in_specs, args, name, scratch=(), limit=8):
    return pl.pallas_call(
        kernel,
        out_shape=outs,
        in_specs=in_specs,
        out_specs=[VMEM] * len(outs) if isinstance(outs, list) else VMEM,
        scratch_shapes=list(scratch),
        compiler_params=pltpu.CompilerParams(vmem_limit_bytes=limit << 20),
        cost_estimate=pl.CostEstimate(flops=COST[name], bytes_accessed=0, transcendentals=0),
        name=name,
    )(*args)


def hint_kernel(mark):
    mark[...] = jnp.zeros_like(mark)


def label_kernel(n, mark, panel, low, own, out, maps, labelled):
    maps[...] = jnp.zeros_like(maps)
    for line, ref in ((LOW, low), (OWN, own), (OUT, out)):
        maps[line : line + 1, 0 : ref.shape[2]] = ref[0]
    labelled[0:n] = panel[...]
    labelled[n:] = jnp.zeros((LINES, labelled.shape[1]), f32)
    labelled[n:, 0:LANES] = maps[...].astype(f32)


def pair_kernel(n, after, own, other, joined, maps):
    joined[0:n] = own[...]
    joined[n : 2 * n] = other[0:n]
    maps[...] = other[n:, 0:LANES].astype(i32)


def pack_kernel(own, other, maps):
    maps[...] = jnp.zeros_like(maps)
    maps[0:OTHER] = own[0:OTHER]
    maps[OTHER : 2 * OTHER] = other[0:OTHER]


def merge_kernel(n, after, near, far, along, joined):
    for k, ref in enumerate((along, near, far)):
        joined[2 * n * k : 2 * n * (k + 1)] = ref[...]


def mark_kernel(after, along, mark):
    mark[...] = along[0:LINES, 0:LANES]


def scalars(values, count):
    return [values[0, u] for u in range(count)]


def send_kernel(plan, turned, maps, maps_met, mine, met, sent):
    line = lambda ref, k: jnp.broadcast_to(ref[k : k + 1, :], (LINES, LANES))
    through = lambda targets, slots: jnp.take_along_axis(targets, slots, axis=1, mode="promise_in_bounds")
    if plan.balanced:
        odd = plan.is_odd() == turned
        own_slots = jnp.where(odd, through(line(maps, OTHER + OWN), line(maps, LOW)), line(maps, OUT))
        target = jnp.where(odd, line(maps_met, OTHER + OUT), line(maps, OUT))
        met_slots = through(target, line(maps_met, LOW))
        sent[...] = jnp.zeros_like(sent)
        for u, slot in enumerate(scalars(own_slots, plan.slots)):
            sent[slot] += mine[0, 0, u]
    else:
        met_slots = line(maps_met, LOW)
        sent[...] = mine[0, 0]
    for u, slot in enumerate(scalars(met_slots, plan.slots)):
        sent[slot] += met[0, 0, u]


def tiles_kernel(plan, turned, maps, maps_met, mine, met, *refs):
    parts, tiles = refs[:-1], refs[-1]
    odd = plan.is_odd() == turned
    tiles[...] = jnp.zeros_like(tiles)
    for u in range(plan.slots):
        tiles[maps[OWN, u]] += mine[0, 0, u]
    for u in range(plan.slots):
        slot = maps[OWN, maps_met[LOW, u]]
        if plan.balanced:
            slot = jnp.where(odd, maps_met[OUT, u], slot)
        tiles[slot] += met[0, 0, u]
    count = plan.tiles // len(parts)
    for k, ref in enumerate(parts):
        ref[...] = tiles[k * count : (k + 1) * count]


def part_kernel(plan, places, upper, lower, *refs):
    part, left, right = refs[-3:]
    n, size = plan.part_rows, plan.size
    odd = plan.is_odd()

    def lay(parity):
        for ref, chunks in zip(refs, places[parity]):
            for k, (kind, offset) in ((k, place) for k, chunk in enumerate(chunks) for place in chunk):
                to, me = (left, lax.axis_index("cube")) if kind == ROW else (right, lax.axis_index("blk"))
                at = lax.bitwise_xor(me, i32(offset))
                to[pl.ds(pl.multiple_of(at * n, n), n), :] = ref[k * n : (k + 1) * n]

    if places[0] == places[1]:
        lay(0)
    else:
        pl.when(jnp.logical_not(odd))(functools.partial(lay, 0))
        pl.when(odd)(functools.partial(lay, 1))

    def strip(i, tiles, k):
        panel = left[pl.ds(pl.multiple_of(i * size, size), size), :]
        for j in range(plan.across):
            product = lax.dot_general(
                panel,
                right[j * size : (j + 1) * size, :],
                (((1,), (1,)), ((), ())),
                precision=lax.Precision.HIGHEST,
                preferred_element_type=f32,
            )
            part[pl.ds(pl.multiple_of(i * size, size), size), j * size : (j + 1) * size] = (
                tiles[k * plan.across + j] - product
            )

    half = plan.rows // size // 2
    pl.loop(0, half)(lambda i: strip(i, upper, i))
    pl.loop(0, half)(lambda i: strip(half + i, lower, i))


def last_kernel(plan, *refs):
    size, across = plan.size, plan.across
    if plan.balanced:
        part, tiles, result = refs
    else:
        maps, part, got, result, tiles = refs
        tiles[...] = jnp.zeros_like(tiles)
        for u in range(plan.slots):
            tiles[maps[OTHER + OUT, u]] += got[u]
    for t in range(plan.tiles):
        i, j = t // across, t % across
        at = (slice(i * size, (i + 1) * size), slice(j * size, (j + 1) * size))
        result[at] = part[at] + tiles[t]


def after(first, *then):
    return lax.optimization_barrier((first, *then))[1:]


def add_sent(plan, turned, maps, updates, met):
    return call(
        functools.partial(send_kernel, plan, turned),
        jax.ShapeDtypeStruct(updates.shape[2:], f32),
        [VMEM] * 4,
        (*maps, updates, met),
        "send",
    )


def add_tiles(plan, turned, maps, updates, met):
    return call(
        functools.partial(tiles_kernel, plan, turned),
        [jax.ShapeDtypeStruct((plan.tiles // 2, plan.size, plan.size), f32)] * 2,
        [SMEM] * 2 + [VMEM] * 2,
        (*maps, updates, met),
        "tiles",
        [pltpu.VMEM((plan.tiles, plan.size, plan.size), f32)],
        limit=24,
    )


def add_part(plan, places, tiles, panels):
    return call(
        functools.partial(part_kernel, plan, places),
        jax.ShapeDtypeStruct((plan.rows, plan.cols), f32),
        [VMEM] * (2 + len(panels)),
        (*tiles, *panels),
        "part",
        [pltpu.VMEM((plan.rows, plan.depth), f32), pltpu.VMEM((plan.cols, plan.depth), f32)],
        limit=40,
    )


def add_last(plan, maps, part, got):
    return call(
        functools.partial(last_kernel, plan),
        jax.ShapeDtypeStruct((plan.rows, plan.cols), f32),
        [SMEM] * len(maps) + [VMEM] * 2,
        (*maps, part, got),
        "last",
        [] if plan.balanced else [pltpu.VMEM((plan.tiles, plan.size, plan.size), f32)],
        limit=40,
    )


def any_mesh(plan, updates, pivot_panel, map_low, map_own, map_out):
    met = plan.swap(updates, 0)
    own_maps = jnp.concatenate([map_low[0], map_own[0], map_out[0]])
    own_maps = jnp.pad(own_maps, ((0, 0), (0, LANES - plan.slots)))
    maps = jnp.concatenate([own_maps, plan.swap(own_maps, 1)])
    maps_met = plan.swap(maps, 0)
    got = plan.swap(add_sent(plan, True, [maps, maps_met], updates, met), 1)
    panels, places = [pivot_panel], [[[(ROW, 0), (COL, 0)]]]
    for c in range(1, plan.cubes):
        panels.append(plan.move(pivot_panel, (c, 0), (c, 0)))
        places.append([[(ROW, c)]])
    for b in range(1, plan.blks):
        panels.append(plan.move(pivot_panel, (0, b), (0, b)))
        places.append([[(COL, b)]])
    tiles = add_tiles(plan, True, (maps, maps_met), updates, met)
    part = add_part(plan, (places, places), tiles, panels)
    return add_last(plan, [] if plan.balanced else [maps], part, got)


def four_by_eight(plan, updates, pivot_panel, map_low, map_own, map_out):
    n, depth = plan.part_rows, plan.depth
    x, y = plan.low, plan.up
    shape = jax.ShapeDtypeStruct
    sibling = lambda shard: plan.move(shard, (0, 1), (0, 1))
    met = plan.cross(updates, 0)
    mark = call(hint_kernel, shape((LINES, LANES), f32), [], (), "hint")
    lines = shape((LINES, LANES), i32)
    own_maps, labelled = call(
        functools.partial(label_kernel, n),
        [lines, shape((n + LINES, depth), f32)],
        [VMEM] * 5,
        (mark, pivot_panel, map_low, map_own, map_out),
        "label",
    )
    other_maps = plan.cross(own_maps, 1)
    twin = sibling(updates)
    pair, twin_maps = call(
        functools.partial(pair_kernel, n),
        [shape((2 * n, depth), f32), lines],
        [VMEM] * 3,
        (twin, pivot_panel, sibling(labelled)),
        "pair",
    )
    along = plan.move(pair, (0, 4), (0, 6))
    maps = call(pack_kernel, lines, [VMEM] * 2, (twin_maps, other_maps), "pack")
    maps_met = plan.move(maps, (y, 0), (x, 0))
    (pair_late,) = after(maps, pair)
    near = plan.move(pair_late, (x, 0), (y, 0))
    far = plan.move(pair_late, (x ^ y, 0), (0, 2))

    sent = add_sent(plan, False, [maps, maps_met], twin, met)
    got = plan.move(sent, (x, 1), (y, 1))
    sent, twin_late, met_late = lax.optimization_barrier((sent, twin, met))
    tiles = add_tiles(plan, False, (maps, maps_met), twin_late, met_late)

    mark = call(mark_kernel, shape((LINES, LANES), f32), [VMEM] * 2, (tiles[0], along), "mark")
    far, near, mark = lax.optimization_barrier((far, near, mark))
    merged = call(
        functools.partial(merge_kernel, n),
        shape((6 * n, depth), f32),
        [VMEM] * 4,
        (mark, near, far, along),
        "merge",
    )
    shared = sibling(merged)
    own = [[(ROW, 0), (COL, 0)], [(COL, 1)]]
    cols = lambda b: [[(COL, b)], [(COL, b ^ 1)]]
    even = [own, cols(4) + [[(ROW, x)], [], [(ROW, x ^ y)], []], cols(7) + [[], [(ROW, y)]] + cols(3)]
    odd = [own, cols(6) + [[(ROW, y)], []] + cols(2), cols(5) + [[], [(ROW, x)], [], [(ROW, x ^ y)]]]
    panels = [pair, merged, shared]
    part = add_part(plan, (even, odd), [sibling(t) for t in tiles], panels)
    return add_last(plan, [], part, got)


def local(updates, *rest):
    plan = Plan(updates, rest[0])
    known = plan.balanced and plan.cubes == 4 and plan.blks == 8
    result = (four_by_eight if known else any_mesh)(plan, updates, *rest)
    return result.reshape(plan.cubes, 1, plan.part_rows, plan.cols)


def solution(mesh):
    placed = (
        P("cube", "blk", None, None, None),
        P(("cube", "blk"), None),
        P("cube", "blk", None),
        P("cube", "blk", None),
        P("cube", "blk", None),
    )
    return jax.shard_map(
        local, mesh=mesh, in_specs=placed, out_specs=P(None, "blk", None, "cube"), check_vma=False
    )
```

```python
import functools

import jax
import jax.numpy as jnp
from jax import lax
from jax.experimental import pallas as pl
from jax.experimental.pallas import tpu as pltpu
from jax.sharding import PartitionSpec as P

AXES = ("cube", "blk")
VMEM = pl.BlockSpec(memory_space=pltpu.VMEM)
SMEM = pl.BlockSpec(memory_space=pltpu.SMEM)
ROW, COL = "row", "col"
LINES, LANES = 8, 128
LOW, OWN, OUT, OTHER = 0, 1, 2, 3
f32, i32 = jnp.float32, jnp.int32
COST = dict(hint=1 << 33, label=0, pair=0, pack=0, send=1 << 30, tiles=0, mark=34 << 25, merge=0, part=0, last=0)


class Plan:
    def __init__(self, updates, pivot_panel):
        self.slots, self.size = updates.shape[2], updates.shape[3]
        self.part_rows, self.depth = pivot_panel.shape
        self.cubes, self.blks = lax.axis_size("cube"), lax.axis_size("blk")
        self.rows, self.cols = self.cubes * self.part_rows, self.blks * self.part_rows
        self.across = self.cols // self.size
        self.tiles = self.rows // self.size * self.across
        bit_count = self.cubes.bit_length() - 1
        self.low, self.up = 1 << (bit_count - 2), 1 << (bit_count - 1)
        self.balanced = self.tiles <= self.slots

    def offset(self, b, stage):
        turned = self.balanced and b % 2 == 1
        return self.up if turned == (stage == 0) else self.low

    def move(self, shard, even, odd):
        pairs = []
        for c in range(self.cubes):
            for b in range(self.blks):
                if (odd if b % 2 else even) is None:
                    continue
                dc, db = odd if b % 2 else even
                pairs.append((c * self.blks + b, (c ^ dc) * self.blks + (b ^ db)))
        return lax.ppermute(shard, AXES, pairs)

    def swap(self, shard, stage):
        return self.move(shard, (self.offset(0, stage), 0), (self.offset(1, stage), 0))

    def cross(self, shard, stage):
        return self.move(shard, (self.offset(0, stage), 1), (self.offset(1, stage), 1))

    def is_odd(self):
        return lax.rem(lax.axis_index("blk"), 2) == 1


def call(kernel, outs, in_specs, args, name, scratch=(), limit=8):
    return pl.pallas_call(
        kernel,
        out_shape=outs,
        in_specs=in_specs,
        out_specs=[VMEM] * len(outs) if isinstance(outs, list) else VMEM,
        scratch_shapes=list(scratch),
        compiler_params=pltpu.CompilerParams(vmem_limit_bytes=limit << 20),
        cost_estimate=pl.CostEstimate(flops=COST[name], bytes_accessed=0, transcendentals=0),
        name=name,
    )(*args)


def hint_kernel(mark):
    mark[...] = jnp.zeros_like(mark)


def label_kernel(n, mark, panel, low, own, out, maps, labelled):
    maps[...] = jnp.zeros_like(maps)
    for line, ref in ((LOW, low), (OWN, own), (OUT, out)):
        maps[line : line + 1, 0 : ref.shape[2]] = ref[0]
    labelled[0:n] = panel[...]
    labelled[n:] = jnp.zeros((LINES, labelled.shape[1]), f32)
    labelled[n:, 0:LANES] = maps[...].astype(f32)


def pair_kernel(n, after, own, other, joined, maps):
    joined[0:n] = own[...]
    joined[n : 2 * n] = other[0:n]
    maps[...] = other[n:, 0:LANES].astype(i32)


def pack_kernel(own, other, maps):
    maps[...] = jnp.zeros_like(maps)
    maps[0:OTHER] = own[0:OTHER]
    maps[OTHER : 2 * OTHER] = other[0:OTHER]


def merge_kernel(n, after, near, far, along, joined):
    for k, ref in enumerate((along, near, far)):
        joined[2 * n * k : 2 * n * (k + 1)] = ref[...]


def mark_kernel(after, along, mark):
    mark[...] = along[0:LINES, 0:LANES]


def scalars(values, count):
    return [values[0, u] for u in range(count)]


def send_kernel(plan, turned, maps, maps_met, mine, met, sent):
    line = lambda ref, k: jnp.broadcast_to(ref[k : k + 1, :], (LINES, LANES))
    through = lambda targets, slots: jnp.take_along_axis(targets, slots, axis=1, mode="promise_in_bounds")
    if plan.balanced:
        odd = plan.is_odd() == turned
        own_slots = jnp.where(odd, through(line(maps, OTHER + OWN), line(maps, LOW)), line(maps, OUT))
        target = jnp.where(odd, line(maps_met, OTHER + OUT), line(maps, OUT))
        met_slots = through(target, line(maps_met, LOW))
        sent[...] = jnp.zeros_like(sent)
        for u, slot in enumerate(scalars(own_slots, plan.slots)):
            sent[slot] += mine[0, 0, u]
    else:
        met_slots = line(maps_met, LOW)
        sent[...] = mine[0, 0]
    for u, slot in enumerate(scalars(met_slots, plan.slots)):
        sent[slot] += met[0, 0, u]


def tiles_kernel(plan, turned, maps, maps_met, mine, met, *refs):
    parts, tiles = refs[:-1], refs[-1]
    odd = plan.is_odd() == turned
    tiles[...] = jnp.zeros_like(tiles)
    for u in range(plan.slots):
        tiles[maps[OWN, u]] += mine[0, 0, u]
    for u in range(plan.slots):
        slot = maps[OWN, maps_met[LOW, u]]
        if plan.balanced:
            slot = jnp.where(odd, maps_met[OUT, u], slot)
        tiles[slot] += met[0, 0, u]
    count = plan.tiles // len(parts)
    for k, ref in enumerate(parts):
        ref[...] = tiles[k * count : (k + 1) * count]


def part_kernel(plan, places, upper, lower, *refs):
    part, left, right = refs[-3:]
    n, size = plan.part_rows, plan.size
    odd = plan.is_odd()

    def lay(parity):
        for ref, chunks in zip(refs, places[parity]):
            for k, (kind, offset) in ((k, place) for k, chunk in enumerate(chunks) for place in chunk):
                to, me = (left, lax.axis_index("cube")) if kind == ROW else (right, lax.axis_index("blk"))
                at = lax.bitwise_xor(me, i32(offset))
                to[pl.ds(pl.multiple_of(at * n, n), n), :] = ref[k * n : (k + 1) * n]

    if places[0] == places[1]:
        lay(0)
    else:
        pl.when(jnp.logical_not(odd))(functools.partial(lay, 0))
        pl.when(odd)(functools.partial(lay, 1))

    def strip(i, tiles, k):
        panel = left[pl.ds(pl.multiple_of(i * size, size), size), :]
        for j in range(plan.across):
            product = lax.dot_general(
                panel,
                right[j * size : (j + 1) * size, :],
                (((1,), (1,)), ((), ())),
                precision=lax.Precision.HIGHEST,
                preferred_element_type=f32,
            )
            part[pl.ds(pl.multiple_of(i * size, size), size), j * size : (j + 1) * size] = (
                tiles[k * plan.across + j] - product
            )

    half = plan.rows // size // 2
    pl.loop(0, half)(lambda i: strip(i, upper, i))
    pl.loop(0, half)(lambda i: strip(half + i, lower, i))


def last_kernel(plan, *refs):
    size, across = plan.size, plan.across
    if plan.balanced:
        part, tiles, result = refs
    else:
        maps, part, got, result, tiles = refs
        tiles[...] = jnp.zeros_like(tiles)
        for u in range(plan.slots):
            tiles[maps[OTHER + OUT, u]] += got[u]
    for t in range(plan.tiles):
        i, j = t // across, t % across
        at = (slice(i * size, (i + 1) * size), slice(j * size, (j + 1) * size))
        result[at] = part[at] + tiles[t]


def after(first, *then):
    return lax.optimization_barrier((first, *then))[1:]


def add_sent(plan, turned, maps, updates, met):
    return call(
        functools.partial(send_kernel, plan, turned),
        jax.ShapeDtypeStruct(updates.shape[2:], f32),
        [VMEM] * 4,
        (*maps, updates, met),
        "send",
    )


def add_tiles(plan, turned, maps, updates, met):
    return call(
        functools.partial(tiles_kernel, plan, turned),
        [jax.ShapeDtypeStruct((plan.tiles // 2, plan.size, plan.size), f32)] * 2,
        [SMEM] * 2 + [VMEM] * 2,
        (*maps, updates, met),
        "tiles",
        [pltpu.VMEM((plan.tiles, plan.size, plan.size), f32)],
        limit=24,
    )


def add_part(plan, places, tiles, panels):
    return call(
        functools.partial(part_kernel, plan, places),
        jax.ShapeDtypeStruct((plan.rows, plan.cols), f32),
        [VMEM] * (2 + len(panels)),
        (*tiles, *panels),
        "part",
        [pltpu.VMEM((plan.rows, plan.depth), f32), pltpu.VMEM((plan.cols, plan.depth), f32)],
        limit=40,
    )


def add_last(plan, maps, part, got):
    return call(
        functools.partial(last_kernel, plan),
        jax.ShapeDtypeStruct((plan.rows, plan.cols), f32),
        [SMEM] * len(maps) + [VMEM] * 2,
        (*maps, part, got),
        "last",
        [] if plan.balanced else [pltpu.VMEM((plan.tiles, plan.size, plan.size), f32)],
        limit=40,
    )


def any_mesh(plan, updates, pivot_panel, map_low, map_own, map_out):
    met = plan.swap(updates, 0)
    own_maps = jnp.concatenate([map_low[0], map_own[0], map_out[0]])
    own_maps = jnp.pad(own_maps, ((0, 0), (0, LANES - plan.slots)))
    maps = jnp.concatenate([own_maps, plan.swap(own_maps, 1)])
    maps_met = plan.swap(maps, 0)
    got = plan.swap(add_sent(plan, True, [maps, maps_met], updates, met), 1)
    panels, places = [pivot_panel], [[[(ROW, 0), (COL, 0)]]]
    for c in range(1, plan.cubes):
        panels.append(plan.move(pivot_panel, (c, 0), (c, 0)))
        places.append([[(ROW, c)]])
    for b in range(1, plan.blks):
        panels.append(plan.move(pivot_panel, (0, b), (0, b)))
        places.append([[(COL, b)]])
    tiles = add_tiles(plan, True, (maps, maps_met), updates, met)
    part = add_part(plan, (places, places), tiles, panels)
    return add_last(plan, [] if plan.balanced else [maps], part, got)


def four_by_eight(plan, updates, pivot_panel, map_low, map_own, map_out):
    n, depth = plan.part_rows, plan.depth
    x, y = plan.low, plan.up
    shape = jax.ShapeDtypeStruct
    sibling = lambda shard: plan.move(shard, (0, 1), (0, 1))
    met = plan.cross(updates, 0)
    mark = call(hint_kernel, shape((LINES, LANES), f32), [], (), "hint")
    lines = shape((LINES, LANES), i32)
    own_maps, labelled = call(
        functools.partial(label_kernel, n),
        [lines, shape((n + LINES, depth), f32)],
        [VMEM] * 5,
        (mark, pivot_panel, map_low, map_own, map_out),
        "label",
    )
    other_maps = plan.cross(own_maps, 1)
    twin = sibling(updates)
    pair, twin_maps = call(
        functools.partial(pair_kernel, n),
        [shape((2 * n, depth), f32), lines],
        [VMEM] * 3,
        (twin, pivot_panel, sibling(labelled)),
        "pair",
    )
    along = plan.move(pair, (0, 2), (0, 6))
    maps = call(pack_kernel, lines, [VMEM] * 2, (twin_maps, other_maps), "pack")
    maps_met = plan.move(maps, (y, 0), (x, 0))
    (pair_late,) = after(maps, pair)
    near = plan.move(pair_late, (x, 0), (0, 4))
    far = plan.move(pair_late, (x ^ y, 0), (y, 0))

    sent = add_sent(plan, False, [maps, maps_met], twin, met)
    got = plan.move(sent, (x, 1), (y, 1))
    sent, twin_late, met_late = lax.optimization_barrier((sent, twin, met))
    tiles = add_tiles(plan, False, (maps, maps_met), twin_late, met_late)

    mark = call(mark_kernel, shape((LINES, LANES), f32), [VMEM] * 2, (tiles[0], along), "mark")
    far, near, mark = lax.optimization_barrier((far, near, mark))
    merged = call(
        functools.partial(merge_kernel, n),
        shape((6 * n, depth), f32),
        [VMEM] * 4,
        (mark, near, far, along),
        "merge",
    )
    shared = sibling(merged)
    own = [[(ROW, 0), (COL, 0)], [(COL, 1)]]
    cols = lambda b: [[(COL, b)], [(COL, b ^ 1)]]
    even = [own, cols(2) + [[(ROW, x)], [], [(ROW, x ^ y)], []], cols(7) + cols(5) + [[], [(ROW, y)]]]
    odd = [own, cols(6) + cols(4) + [[(ROW, y)], []], cols(3) + [[], [(ROW, x)], [], [(ROW, x ^ y)]]]
    panels = [pair, merged, shared]
    part = add_part(plan, (even, odd), [sibling(t) for t in tiles], panels)
    return add_last(plan, [], part, got)


def local(updates, *rest):
    plan = Plan(updates, rest[0])
    known = plan.balanced and plan.cubes == 4 and plan.blks == 8
    result = (four_by_eight if known else any_mesh)(plan, updates, *rest)
    return result.reshape(plan.cubes, 1, plan.part_rows, plan.cols)


def solution(mesh):
    placed = (
        P("cube", "blk", None, None, None),
        P(("cube", "blk"), None),
        P("cube", "blk", None),
        P("cube", "blk", None),
        P("cube", "blk", None),
    )
    return jax.shard_map(
        local, mesh=mesh, in_specs=placed, out_specs=P(None, "blk", None, "cube"), check_vma=False
    )
```
